32 devices in a mesh: sec: 8 (over y, x, core), tile: 4 (over z).
Axes of the slice: x: 2, y: 2, z: 4, core: 2. Of those that a mesh axis runs over, the one named last changes fastest.
Arguments:
- descriptors: bfloat16 [16, 192, 128, 128], P('sec', 'tile'), may hold values from -8 to 8
- partner_step: int32 [16], replicated, may hold values from 0 to 2, as said below
Outputs:
- flow: float32 [16, 2, 192, 128], P('sec', None, 'tile')
The draws below stay inside these ranges and needn't reach their ends.
Inputs may be any that keep to these rules, and one draw needn't show every extreme that they name: Every section is sound or damaged. partner_step is 0 for a damaged section; for a sound section it is the distance to the next sound section, or 0 where no sound section lies within 2 ahead inside the stack.
All inputs are finite; a program needn't handle non-finite values.
Results may differ from the reference program's by a relative error of at most 0.0003.
Values may be sent and summed in bfloat16 or wider, within the bound.
A program may use at most 64 MiB of HBM per device.

```python
import math
import jax
import jax.numpy as jnp
from jax import lax

CHANNELS = 128
COLS = 128
WIN = 4
POOL = 8
SKIP = 2
SECTIONS = 16
ROWS = 192


def section_offsets(key):
    moves = jax.random.randint(key, (SECTIONS, 2), -1, 2)
    return jnp.cumsum(moves, axis=0).astype(jnp.int32)


def draw_descriptors(key, part):
    key_noise = jax.random.fold_in(key, 11)
    key_common = jax.random.fold_in(key, 12)
    key_rough = jax.random.fold_in(key, 14)
    key_offsets = jax.random.fold_in(key, 15)
    offsets = section_offsets(key_offsets)
    common = jax.random.normal(key_common, (ROWS, COLS, CHANNELS), jnp.float32)
    ramp = 0.5 + jnp.arange(ROWS, dtype=jnp.float32) / ROWS
    rough = jax.random.uniform(key_rough, (ROWS,), jnp.float32, 0.5, 1.5)
    target = jnp.minimum(4.0, 2560.0 / jnp.sqrt(jnp.float32(CHANNELS * ROWS * COLS)))
    strength = jnp.sqrt(target * ramp * rough)
    row_ids = jnp.arange(ROWS, dtype=jnp.int32)
    col_ids = jnp.arange(COLS, dtype=jnp.int32)

    def one_section(index):
        rows_from = (row_ids - POOL * offsets[index, 0]) % ROWS
        cols_from = (col_ids - POOL * offsets[index, 1]) % COLS
        pattern = jnp.take(jnp.take(common, rows_from, axis=0), cols_from, axis=1)
        section_key = jax.random.fold_in(key_noise, index)
        noise_part = jax.random.normal(section_key, (ROWS, COLS, CHANNELS), jnp.float32)
        drawn = jnp.clip(noise_part + strength[:, None, None] * pattern, -8.0, 8.0)
        return drawn.astype(jnp.bfloat16)
    return lax.map(one_section, jnp.arange(SECTIONS, dtype=jnp.int32))


def draw_partner_step(key, part):
    intact = (jax.random.randint(jax.random.fold_in(key, 21), (SECTIONS,), 0, 5) > 0).astype(jnp.int32)
    intact = intact.at[0].set(1).at[1].set(0).at[2].set(1)
    distance = jnp.zeros((SECTIONS,), jnp.int32)
    for ahead in range(SKIP, 0, -1):
        intact_ahead = jnp.concatenate([intact[ahead:], jnp.zeros((ahead,), jnp.int32)])
        distance = jnp.where(intact_ahead == 1, ahead, distance)
    return jnp.where(intact == 1, distance, 0).astype(jnp.int32)


def setup_inputs(seed: int = 0) -> dict:
    splits = jax.random.split(jax.random.key(seed), 3)
    return {
        "descriptors": draw_descriptors(jax.random.fold_in(splits[2], 71), 0),
        "partner_step": draw_partner_step(jax.random.fold_in(splits[2], 71), 0),
    }


prior_weight = 0.25

def pool_plane(section_plane):
    height, width, depth = section_plane.shape
    summed = lax.optimization_barrier(jnp.sum(section_plane.reshape(height // POOL, POOL, width // POOL, POOL, depth).astype(jnp.float32), axis=(1, 3)))
    pooled = (summed / (POOL * POOL)).astype(jnp.bfloat16)
    return lax.optimization_barrier(pooled).astype(jnp.float32)

def soft_flow(scores, row_offsets, col_offsets):
    highest = lax.optimization_barrier(jnp.max(scores, axis=0, keepdims=True))
    weights = jnp.exp(scores - highest)
    totals = lax.optimization_barrier(jnp.sum(weights, axis=0))
    return (lax.optimization_barrier(jnp.sum(weights * row_offsets, axis=0)) / totals, lax.optimization_barrier(jnp.sum(weights * col_offsets, axis=0)) / totals)

def reference(descriptors, partner_step):
    window_side = 2 * WIN + 1
    offset_ids = jnp.arange(window_side * window_side, dtype=jnp.int32)
    row_offsets = (offset_ids // window_side - WIN).astype(jnp.float32)
    col_offsets = (offset_ids % window_side - WIN).astype(jnp.float32)
    section_ids = jnp.arange(SECTIONS, dtype=jnp.int32)
    partner = jnp.minimum(section_ids + partner_step, SECTIONS - 1).astype(jnp.int32)

    def pair_flow(section):
        fixed_block = lax.dynamic_index_in_dim(descriptors, section, 0, keepdims=False)
        moving = lax.dynamic_index_in_dim(descriptors, partner[section], 0, keepdims=False)
        fixed_coarse = pool_plane(fixed_block)
        moving_coarse = pool_plane(moving)
        coarse_rows, coarse_cols = (fixed_coarse.shape[0], fixed_coarse.shape[1])
        coarse_padded = jnp.pad(moving_coarse, ((WIN, WIN), (WIN, WIN), (0, 0)))
        coarse_scores = jnp.stack([jnp.sum(fixed_coarse * coarse_padded[row_off:row_off + coarse_rows, col_off:col_off + coarse_cols]) for row_off in range(window_side) for col_off in range(window_side)])
        coarse_scores = coarse_scores / math.sqrt(CHANNELS * coarse_rows * coarse_cols)
        shift_row, shift_col = soft_flow(coarse_scores, row_offsets, col_offsets)
        fixed_plane = fixed_block.astype(jnp.float32)
        moving_padded = jnp.pad(moving.astype(jnp.float32), ((WIN, WIN), (WIN, WIN), (0, 0)))
        correlation = jnp.stack([lax.optimization_barrier(jnp.sum(fixed_plane * moving_padded[row_off:row_off + ROWS, col_off:col_off + COLS], axis=-1)) for row_off in range(window_side) for col_off in range(window_side)])
        prior_term = (row_offsets - shift_row) ** 2 + (col_offsets - shift_col) ** 2
        scores = correlation * (1.0 / math.sqrt(CHANNELS)) - prior_weight * prior_term[:, None, None]
        flow_row, flow_col = soft_flow(scores, row_offsets[:, None, None], col_offsets[:, None, None])
        paired = partner_step[section] > 0
        return jnp.where(paired, jnp.stack([flow_row, flow_col]), jnp.float32(0.0))
    return lax.map(pair_flow, section_ids)
```

```python
import functools
import math

import jax
import jax.numpy as jnp
from jax import lax
from jax.experimental import pallas as pl
from jax.experimental.pallas import tpu as pltpu
from jax.sharding import PartitionSpec as P

WIN = 4
POOL = 8
SIDE = 2 * WIN + 1
PRIOR = 0.25
LOG2E = math.log2(math.e)
BAND = 32
LOW = -1e30


def coarse_shift(fixed_ref, moving_ref, count):
    cols = fixed_ref.shape[1]
    lanes = 12 * BAND

    def step(y, total):
        window = moving_ref[pl.ds(y, 12)].reshape(lanes, fixed_ref.shape[2])
        return total + lax.dot_general(
            fixed_ref[y], window, (((1,), (1,)), ((), ())), preferred_element_type=jnp.float32
        )

    table = lax.fori_loop(0, count, step, jnp.zeros((cols, lanes), jnp.float32))
    row = lax.broadcasted_iota(jnp.int32, (cols, lanes), 0)
    for bit in (1, 2, 4, 8):
        table = jnp.where((row & bit) != 0, pltpu.roll(table, lanes - bit, 1), table)
    scores = jnp.sum(table, axis=0, keepdims=True) * (
        1.0 / math.sqrt(fixed_ref.shape[2] * count * cols)
    )
    lane = lax.broadcasted_iota(jnp.int32, (1, lanes), 1) + BAND // 2
    lane = jnp.where(lane >= lanes, lane - lanes, lane)
    dy = (lane // BAND) - WIN
    dx = (lane % BAND) - BAND // 2
    valid = (dy <= WIN) & (jnp.abs(dx) <= WIN)
    scores = jnp.where(valid, scores, LOW)
    weights = jnp.exp(scores - jnp.max(scores, axis=1, keepdims=True))
    total = jnp.sum(weights, axis=1, keepdims=True)
    return (
        jnp.sum(weights * dy.astype(jnp.float32), axis=1, keepdims=True) / total,
        jnp.sum(weights * dx.astype(jnp.float32), axis=1, keepdims=True) / total,
    )


def fill_prior(prior_ref, shift_row, shift_col):
    shape = (256, 128)
    at = lax.broadcasted_iota(jnp.int32, shape, 0)
    cell = lax.broadcasted_iota(jnp.int32, shape, 1)
    dy = (at // 16) - (cell // 16) - WIN
    dx = (at % 16) - (cell % 8) - WIN
    valid = (jnp.abs(dy) <= WIN) & (jnp.abs(dx) <= WIN)
    far = (dy.astype(jnp.float32) - shift_row) ** 2 + (dx.astype(jnp.float32) - shift_col) ** 2
    prior_ref[...] = jnp.where(valid, far * (-PRIOR * LOG2E), LOW)


def widen_row(wide_ref, at, row):
    row = row.astype(jnp.float32)
    edge = jnp.zeros((WIN, row.shape[1]), jnp.float32)
    left = jnp.concatenate([edge, row[:-WIN]], axis=0)
    right = jnp.concatenate([row[WIN:], edge], axis=0)
    wide_ref[at] = jnp.concatenate([left, right], axis=1).astype(jnp.bfloat16)


def tile_flow(window, fixed, prior_ref):
    cell = lax.broadcasted_iota(jnp.int32, fixed.shape, 0)
    first = ((cell % 16) < 8).astype(jnp.float32).astype(jnp.bfloat16)
    both = jnp.concatenate([fixed * first, fixed * (jnp.bfloat16(1.0) - first)], axis=1)
    corr = lax.dot_general(
        window, both, (((1,), (1,)), ((), ())), preferred_element_type=jnp.float32
    )
    scores = corr * (LOG2E / math.sqrt(fixed.shape[1])) + prior_ref[...]
    weights = jnp.exp2(scores - jnp.max(scores, axis=0, keepdims=True)).reshape(16, 16, 128)
    down = weights[15]
    rows = down
    for at in range(14, 0, -1):
        down = down + weights[at]
        rows = rows + down
    down = down + weights[0]
    inverse = 1.0 / jnp.sum(down, axis=0, keepdims=True)
    at = lax.broadcasted_iota(jnp.int32, (16, 128), 0).astype(jnp.float32)
    cell = lax.broadcasted_iota(jnp.int32, (1, 128), 1)
    flow_row = jnp.sum(rows, axis=0, keepdims=True) * inverse
    flow_col = jnp.sum(down * at, axis=0, keepdims=True) * inverse
    return (
        flow_row - ((cell // 16) + WIN).astype(jnp.float32),
        flow_col - ((cell % 8) + WIN).astype(jnp.float32),
    )


def pair_kernel(fixed_ref, low_ref, moving_ref, high_ref, fixed_all, moving_all, out_ref, wide, prior):
    rows = fixed_ref.shape[0]
    groups = fixed_ref.shape[1] // 16
    shift_row, shift_col = coarse_shift(fixed_all, moving_all, fixed_all.shape[0])
    fill_prior(prior, shift_row, shift_col)
    for r in range(WIN):
        widen_row(wide, r, low_ref[r])
        widen_row(wide, rows + WIN + r, high_ref[r])

    def widen(r, carry):
        widen_row(wide, r + WIN, moving_ref[r])
        return carry

    lax.fori_loop(0, rows, widen, 0)

    def group(g, carry):
        top = pl.multiple_of(g * 8, 8)
        flow_rows, flow_cols = [], []
        for j in range(groups):
            window = wide[pl.ds(top, 16), 16 * j : 16 * j + 16, :].reshape(256, 256)
            fixed = fixed_ref[pl.ds(top, 8), 16 * j : 16 * j + 16, :].reshape(128, 128)
            flow_row, flow_col = tile_flow(window, fixed, prior)
            flow_rows.append(flow_row)
            flow_cols.append(flow_col)
        out_ref[0, g] = jnp.concatenate(flow_rows, axis=0)
        out_ref[1, g] = jnp.concatenate(flow_cols, axis=0)
        return carry

    lax.fori_loop(0, rows // 8, group, 0)


def pair_flow(fixed, low, moving, high, fixed_all, moving_all):
    rows, cols, depth = fixed.shape
    spec = pl.BlockSpec(memory_space=pltpu.VMEM)
    return pl.pallas_call(
        pair_kernel,
        out_shape=jax.ShapeDtypeStruct((2, rows // 8, cols // 16, 128), jnp.float32),
        in_specs=[spec] * 6,
        out_specs=spec,
        scratch_shapes=[
            pltpu.VMEM((rows + 2 * WIN, cols, 2 * depth), jnp.bfloat16),
            pltpu.VMEM((256, 128), jnp.float32),
        ],
        compiler_params=pltpu.CompilerParams(vmem_limit_bytes=40 * 2**20),
        cost_estimate=pl.CostEstimate(
            flops=2 * 256 * 256 * rows * cols, bytes_accessed=2**22, transcendentals=256 * rows * cols
        ),
    )(fixed, low, moving, high, fixed_all, moving_all)


def pool_block(block):
    count, height, width, depth = block.shape
    summed = jnp.sum(
        block.reshape(count, height // POOL, POOL, width // POOL, POOL, depth),
        axis=(2, 4),
        dtype=jnp.float32,
    )
    return (summed / (POOL * POOL)).astype(jnp.bfloat16)


def body(descriptors, partner_step):
    sections, row_count, col_count, depth = descriptors.shape
    sec_index = lax.axis_index("sec")
    first_sec = sec_index * sections
    own_steps = lax.dynamic_slice_in_dim(partner_step, first_sec, sections)
    prev_start = jnp.maximum(first_sec - sections, 0)
    prev_steps = lax.dynamic_slice_in_dim(partner_step, prev_start, sections)
    reach = prev_start + jnp.arange(sections, dtype=jnp.int32) + prev_steps - first_sec
    crossing = (sec_index > 0) & (prev_steps > 0) & (reach >= 0)
    chosen = jnp.sum(jnp.where(crossing, reach, 0))
    sender = jnp.where(own_steps[1] > 0, 1, 0)

    sec_count, tile_count = lax.axis_size("sec"), lax.axis_size("tile")
    back = [(i, i - 1) for i in range(1, sec_count)]
    up = [(i, i + 1) for i in range(tile_count - 1)]
    down = [(b, a) for a, b in up]
    pick = lambda a, k: jnp.where(k == 0, a[0], a[1])
    outgoing = pick(descriptors, chosen)
    incoming = lax.ppermute(outgoing, "sec", back)
    coarse = lax.all_gather(pool_block(descriptors), "tile", axis=1, tiled=True)
    low = lax.ppermute(descriptors[:, row_count - WIN :], "tile", up)
    high = lax.ppermute(descriptors[:, :WIN], "tile", down)
    edges = lax.ppermute(jnp.concatenate([pick(low, chosen), pick(high, chosen)]), "sec", back)
    coarse_in = lax.ppermute(pick(coarse, chosen), "sec", back)
    widen = lambda a: jnp.pad(a, ((WIN, 12 - WIN), (0, BAND - a.shape[1]), (0, 0)))

    near = pair_flow(descriptors[0], low[1], descriptors[1], high[1], coarse[0], widen(coarse[1]))
    far = pair_flow(
        pick(descriptors, sender), edges[:WIN], incoming, edges[WIN:], pick(coarse, sender), widen(coarse_in)
    )
    flow = jnp.stack(
        [
            jnp.where(own_steps[0] == 1, near, jnp.where(own_steps[0] == 2, far, 0.0)),
            jnp.where(own_steps[1] > 0, far, 0.0),
        ]
    )
    flow = flow.reshape(sections, 2, row_count // 8, col_count // 16, 8, 16)
    return flow.transpose(0, 1, 2, 4, 3, 5).reshape(sections, 2, row_count, col_count)


def solution(mesh):
    return jax.shard_map(
        body,
        mesh=mesh,
        in_specs=(P("sec", "tile", None, None), P()),
        out_specs=P("sec", None, "tile", None),
        check_vma=False,
    )
```

```python
import functools
import math

import jax
import jax.numpy as jnp
from jax import lax
from jax.experimental import pallas as pl
from jax.experimental.pallas import tpu as pltpu
from jax.sharding import PartitionSpec as P

WIN = 4
POOL = 8
SIDE = 2 * WIN + 1
PRIOR = 0.25
LOG2E = math.log2(math.e)
BAND = 32
LOW = -1e30


def coarse_shift(fixed_row, padded_ref, count):
    cols, depth = 16, padded_ref.shape[2]
    lanes = 12 * BAND

    def step(y, total):
        window = padded_ref[pl.ds(y, 12)].reshape(lanes, depth)
        return total + lax.dot_general(
            fixed_row(y), window, (((1,), (1,)), ((), ())), preferred_element_type=jnp.float32
        )

    table = lax.fori_loop(0, count, step, jnp.zeros((cols, lanes), jnp.float32))
    row = lax.broadcasted_iota(jnp.int32, (cols, lanes), 0)
    for bit in (1, 2, 4, 8):
        table = jnp.where((row & bit) != 0, pltpu.roll(table, lanes - bit, 1), table)
    scores = jnp.sum(table, axis=0, keepdims=True) * (
        1.0 / math.sqrt(depth * count * cols)
    )
    lane = lax.broadcasted_iota(jnp.int32, (1, lanes), 1) + BAND // 2
    lane = jnp.where(lane >= lanes, lane - lanes, lane)
    dy = (lane // BAND) - WIN
    dx = (lane % BAND) - BAND // 2
    valid = (dy <= WIN) & (jnp.abs(dx) <= WIN)
    scores = jnp.where(valid, scores, LOW)
    weights = jnp.exp(scores - jnp.max(scores, axis=1, keepdims=True))
    total = jnp.sum(weights, axis=1, keepdims=True)
    return (
        jnp.sum(weights * dy.astype(jnp.float32), axis=1, keepdims=True) / total,
        jnp.sum(weights * dx.astype(jnp.float32), axis=1, keepdims=True) / total,
    )


def fill_prior(prior_ref, shift_row, shift_col):
    shape = (256, 128)
    at = lax.broadcasted_iota(jnp.int32, shape, 0)
    cell = lax.broadcasted_iota(jnp.int32, shape, 1)
    dy = (at // 16) - (cell // 16) - WIN
    dx = (at % 16) - (cell % 8) - WIN
    valid = (jnp.abs(dy) <= WIN) & (jnp.abs(dx) <= WIN)
    far = (dy.astype(jnp.float32) - shift_row) ** 2 + (dx.astype(jnp.float32) - shift_col) ** 2
    prior_ref[...] = jnp.where(valid, far * (-PRIOR * LOG2E), LOW)


def widen_row(wide_ref, at, row):
    row = row.astype(jnp.float32)
    edge = jnp.zeros((WIN, row.shape[1]), jnp.float32)
    left = jnp.concatenate([edge, row[:-WIN]], axis=0)
    right = jnp.concatenate([row[WIN:], edge], axis=0)
    wide_ref[at] = jnp.concatenate([left, right], axis=1).astype(jnp.bfloat16)


def tile_flow(window, fixed, prior_ref):
    cell = lax.broadcasted_iota(jnp.int32, fixed.shape, 0)
    first = ((cell % 16) < 8).astype(jnp.float32).astype(jnp.bfloat16)
    both = jnp.concatenate([fixed * first, fixed * (jnp.bfloat16(1.0) - first)], axis=1)
    corr = lax.dot_general(
        window, both, (((1,), (1,)), ((), ())), preferred_element_type=jnp.float32
    )
    scores = corr * (LOG2E / math.sqrt(fixed.shape[1])) + prior_ref[...]
    weights = jnp.exp2(scores - jnp.max(scores, axis=0, keepdims=True)).reshape(16, 16, 128)
    down = weights[15]
    rows = down
    for at in range(14, 0, -1):
        down = down + weights[at]
        rows = rows + down
    down = down + weights[0]
    inverse = 1.0 / jnp.sum(down, axis=0, keepdims=True)
    at = lax.broadcasted_iota(jnp.int32, (16, 128), 0).astype(jnp.float32)
    cell = lax.broadcasted_iota(jnp.int32, (1, 128), 1)
    flow_row = jnp.sum(rows, axis=0, keepdims=True) * inverse
    flow_col = jnp.sum(down * at, axis=0, keepdims=True) * inverse
    return (
        flow_row - ((cell // 16) + WIN).astype(jnp.float32),
        flow_col - ((cell % 8) + WIN).astype(jnp.float32),
    )


def flow_group(wide, fixed_rows, prior, out_ref, g):
    flow_rows, flow_cols = [], []
    top = pl.multiple_of(g * 8, 8)
    for j in range(wide.shape[1] // 16):
        window = wide[pl.ds(top, 16), 16 * j : 16 * j + 16, :].reshape(256, 256)
        fixed = fixed_rows(top, 16 * j).reshape(128, 128)
        flow_row, flow_col = tile_flow(window, fixed, prior)
        flow_rows.append(flow_row)
        flow_cols.append(flow_col)
    out_ref[0, g] = jnp.concatenate(flow_rows, axis=0)
    out_ref[1, g] = jnp.concatenate(flow_cols, axis=0)


def loop(start, stop, step):
    def run(at, carry):
        step(at)
        return carry

    lax.fori_loop(start, stop, run, 0)


def kernel(
    secs, tiles, desc, steps, out,
    sending, incoming, coarse, coarse_out, coarse_in, padded, near_edge, far_edge, wide, prior, near, far,
    main_send, main_recv, near_send, near_recv, far_send, far_recv,
    gather_send, gather_recv, hop_send, hop_recv, spread_send, spread_recv,
):
    rows = desc.shape[1]
    chunks = rows // POOL
    i, t = lax.axis_index("sec"), lax.axis_index("tile")
    own_first, own_second = steps[2 * i], steps[2 * i + 1]
    chosen = jnp.where(steps[jnp.maximum(2 * i - 1, 0)] == 2, 1, 0)
    sender = jnp.where(own_second > 0, 1, 0)
    gives, takes = i > 0, i < secs - 1

    def peer(d):
        return lax.rem(t + d, tiles)

    def remote(src, dst, send, recv, target):
        return pltpu.make_async_remote_copy(
            src_ref=src, dst_ref=dst, send_sem=send, recv_sem=recv,
            device_id=target, device_id_type=pl.DeviceIdType.MESH,
        )

    def main_copy(k):
        part = pl.ds(pl.multiple_of(k * POOL, POOL), POOL)
        return remote(
            sending.at[part], incoming.at[part], main_send.at[k], main_recv.at[k], {"sec": i - 1}
        )

    def gather_copy(d):
        slot = coarse.at[:, t]
        return remote(slot, slot, gather_send.at[d], gather_recv.at[d], {"tile": peer(d)})

    def hop_copy():
        return remote(coarse_out, coarse_in.at[t], hop_send, hop_recv, {"sec": i - 1})

    def spread_copy(d):
        slot = coarse_in.at[t]
        return remote(slot, slot, spread_send.at[d], spread_recv.at[d], {"tile": peer(d)})

    def edge_copy(source, edge, sems, side):
        part = source.at[rows - WIN :] if side == 0 else source.at[:WIN]
        target = t + 1 if side == 0 else t - 1
        return remote(part, edge.at[side], sems[0].at[side], sems[1].at[side], {"tile": target})

    near_sems, far_sems = (near_send, near_recv), (far_send, far_recv)
    near_source = desc.at[1]
    has_low, has_high = t > 0, t < tiles - 1

    def start_edges(source, edge, sems):
        pl.when(has_high)(lambda: edge_copy(source, edge, sems, 0).start())
        pl.when(has_low)(lambda: edge_copy(source, edge, sems, 1).start())

    def finish_edges(source, edge, sems):
        pl.when(has_high)(lambda: edge_copy(source, edge, sems, 0).wait_send())
        pl.when(has_low)(lambda: edge_copy(source, edge, sems, 1).wait_send())

    def receive_edges(source, edge, sems):
        pl.when(has_low)(lambda: edge_copy(source, edge, sems, 0).wait_recv())
        pl.when(has_high)(lambda: edge_copy(source, edge, sems, 1).wait_recv())

        @pl.when(t == 0)
        def _():
            edge[0] = jnp.zeros(edge.shape[1:], edge.dtype)

        @pl.when(t == tiles - 1)
        def _():
            edge[1] = jnp.zeros(edge.shape[1:], edge.dtype)

        for r in range(WIN):
            widen_row(wide, r, edge[0, r])
            widen_row(wide, rows + WIN + r, edge[1, r])

    barrier = pltpu.get_barrier_semaphore()

    def greet(target):
        pl.semaphore_signal(barrier, inc=1, device_id=target, device_id_type=pl.DeviceIdType.MESH)

    for d in range(1, tiles):
        greet({"tile": peer(d)})
    pl.when(gives)(lambda: greet({"sec": i - 1}))
    pl.when(takes)(lambda: greet({"sec": i + 1}))

    def fill(r):
        sending[r] = desc[chosen, r]

    loop(0, rows, fill)
    pl.semaphore_wait(barrier, tiles - 1 + jnp.where(gives, 1, 0) + jnp.where(takes, 1, 0))

    @pl.when(gives)
    def _():
        main_copy(0).start()
        main_copy(chunks - 1).start()

    start_edges(near_source, near_edge, near_sems)

    def pool(k):
        means = []
        for s in range(2):
            summed = desc[s, k * POOL].astype(jnp.float32)
            for r in range(1, POOL):
                summed = summed + desc[s, k * POOL + r].astype(jnp.float32)
            summed = jnp.sum(summed.reshape(16, POOL, summed.shape[1]), axis=1)
            means.append(summed * (1.0 / (POOL * POOL)))
            coarse[s, t, k] = means[s].astype(jnp.bfloat16)
        coarse_out[k] = jnp.where(chosen == 0, means[0], means[1]).astype(jnp.bfloat16)

    loop(0, chunks, pool)
    for d in range(1, tiles):
        gather_copy(d).start()

    @pl.when(gives)
    def _():
        hop_copy().start()
        loop(1, chunks - 1, lambda k: main_copy(k).start())

    total = tiles * chunks
    padded[...] = jnp.zeros(padded.shape, padded.dtype)
    loop(0, rows, lambda r: widen_row(wide, r + WIN, desc[1, r]))
    for d in range(1, tiles):
        gather_copy(d).wait_recv()

    def lay(load):
        for at in range(tiles):
            for k in range(chunks):
                padded[WIN + at * chunks + k, :16] = load(at, k)

    lay(lambda at, k: coarse[1, at, k])
    shift_row, shift_col = coarse_shift(lambda y: coarse[0, y // chunks, y % chunks], padded, total)
    fill_prior(prior, shift_row, shift_col)
    receive_edges(near_source, near_edge, near_sems)
    loop(
        0, chunks,
        lambda g: flow_group(wide, lambda top, col: desc[0, pl.ds(top, 8), col : col + 16, :], prior, near, g),
    )

    @pl.when(takes)
    def _():
        hop_copy().wait_recv()
        for d in range(1, tiles):
            spread_copy(d).start()
        main_copy(0).wait_recv()
        main_copy(chunks - 1).wait_recv()
        start_edges(incoming, far_edge, far_sems)
        for r in range(POOL):
            widen_row(wide, r + WIN, incoming[r])
            widen_row(wide, rows - POOL + r + WIN, incoming[rows - POOL + r])
        for d in range(1, tiles):
            spread_copy(d).wait_recv()
        lay(lambda at, k: coarse_in[at, k])
        shift_row, shift_col = coarse_shift(lambda y: coarse[sender, y // chunks, y % chunks], padded, total)
        fill_prior(prior, shift_row, shift_col)
        receive_edges(incoming, far_edge, far_sems)

        def group(g):
            @pl.when(g < chunks - 2)
            def _():
                main_copy(g + 1).wait_recv()
                first = (g + 1) * POOL
                for r in range(POOL):
                    widen_row(wide, first + r + WIN, incoming[first + r])

            flow_group(wide, lambda top, col: desc[sender, pl.ds(top, 8), col : col + 16, :], prior, far, g)

        loop(0, chunks, group)
        for d in range(1, tiles):
            spread_copy(d).wait_send()
        finish_edges(incoming, far_edge, far_sems)

    @pl.when(i == secs - 1)
    def _():
        far[...] = jnp.zeros(far.shape, far.dtype)

    for c in range(2):
        out[0, c] = jnp.where(own_first == 1, near[c], jnp.where(own_first == 2, far[c], 0.0))
        out[1, c] = jnp.where(own_second > 0, far[c], 0.0)

    for d in range(1, tiles):
        gather_copy(d).wait_send()
    finish_edges(near_source, near_edge, near_sems)

    @pl.when(gives)
    def _():
        hop_copy().wait_send()
        loop(0, chunks, lambda k: main_copy(k).wait_send())


def body(descriptors, partner_step):
    sections, rows, cols, depth = descriptors.shape
    secs, tiles = lax.axis_size("sec"), lax.axis_size("tile")
    chunks = rows // POOL
    narrow = jnp.bfloat16
    dma = pltpu.SemaphoreType.DMA
    result = (2, chunks, cols // 16, 128)
    flow = pl.pallas_call(
        functools.partial(kernel, secs, tiles),
        out_shape=jax.ShapeDtypeStruct((sections,) + result, jnp.float32),
        in_specs=[pl.BlockSpec(memory_space=pltpu.VMEM), pl.BlockSpec(memory_space=pltpu.SMEM)],
        out_specs=pl.BlockSpec(memory_space=pltpu.VMEM),
        scratch_shapes=[
            pltpu.VMEM((rows, cols, depth), narrow),
            pltpu.VMEM((rows, cols, depth), narrow),
            pltpu.VMEM((sections, tiles, chunks, 16, depth), narrow),
            pltpu.VMEM((chunks, 16, depth), narrow),
            pltpu.VMEM((tiles, chunks, 16, depth), narrow),
            pltpu.VMEM((tiles * chunks + 12, BAND, depth), narrow),
            pltpu.VMEM((2, WIN, cols, depth), narrow),
            pltpu.VMEM((2, WIN, cols, depth), narrow),
            pltpu.VMEM((rows + 2 * WIN, cols, 2 * depth), narrow),
            pltpu.VMEM((256, 128), jnp.float32),
            pltpu.VMEM(result, jnp.float32),
            pltpu.VMEM(result, jnp.float32),
            dma((chunks,)), dma((chunks,)), dma((2,)), dma((2,)), dma((2,)), dma((2,)),
            dma((tiles,)), dma((tiles,)), dma, dma, dma((tiles,)), dma((tiles,)),
        ],
        compiler_params=pltpu.CompilerParams(
            vmem_limit_bytes=40 * 2**20, collective_id=0, has_side_effects=True
        ),
        cost_estimate=pl.CostEstimate(
            flops=4 * 256 * 256 * rows * cols, bytes_accessed=2**22, transcendentals=512 * rows * cols
        ),
    )(descriptors, partner_step)
    flow = flow.reshape(sections, 2, chunks, cols // 16, 8, 16)
    return flow.transpose(0, 1, 2, 4, 3, 5).reshape(sections, 2, rows, cols)


def solution(mesh):
    return jax.shard_map(
        body,
        mesh=mesh,
        in_specs=(P("sec", "tile", None, None), P()),
        out_specs=P("sec", None, "tile", None),
        check_vma=False,
    )
```

```python
import functools
import math

import jax
import jax.numpy as jnp
from jax import lax
from jax.experimental import pallas as pl
from jax.experimental.pallas import tpu as pltpu
from jax.sharding import PartitionSpec as P

WIN = 4
POOL = 8
SIDE = 2 * WIN + 1
PRIOR = 0.25
LOG2E = math.log2(math.e)
LOW = -1e30


def coarse_shift(fixed_row, padded_ref, count):
    cols, depth = padded_ref.shape[1:]
    lanes = 16 * cols
    table = jnp.zeros((cols, lanes), jnp.float32)
    for y in range(0, count, 2):
        fixed = jnp.concatenate([fixed_row(y), fixed_row(y + 1)], axis=1)
        window = jnp.concatenate(
            [padded_ref[y + k : y + k + 16].reshape(lanes, depth) for k in (0, 1)], axis=1
        )
        table = table + lax.dot_general(
            fixed, window, (((1,), (1,)), ((), ())), preferred_element_type=jnp.float32
        )
    row = lax.broadcasted_iota(jnp.int32, (cols, lanes), 0)
    lane = lax.broadcasted_iota(jnp.int32, (cols, lanes), 1)
    table = jnp.where(jnp.abs(lane % cols - row) <= WIN, table, 0.0)
    for bit in (1, 2, 4, 8):
        table = jnp.where((row & bit) != 0, pltpu.roll(table, lanes - bit, 1), table)
    scores = jnp.sum(table, axis=0, keepdims=True) * (1.0 / math.sqrt(depth * count * cols))
    lane = lax.broadcasted_iota(jnp.int32, (1, lanes), 1) + cols // 2
    lane = jnp.where(lane >= lanes, lane - lanes, lane)
    dy = (lane // cols) - WIN
    dx = (lane % cols) - cols // 2
    valid = (dy <= WIN) & (jnp.abs(dx) <= WIN)
    scores = jnp.where(valid, scores, LOW)
    weights = jnp.exp(scores - jnp.max(scores, axis=1, keepdims=True))
    total = jnp.sum(weights, axis=1, keepdims=True)
    return (
        jnp.sum(weights * dy.astype(jnp.float32), axis=1, keepdims=True) / total,
        jnp.sum(weights * dx.astype(jnp.float32), axis=1, keepdims=True) / total,
    )


def fill_prior(prior_ref, shift_row, shift_col):
    shape = (256, 128)
    at = lax.broadcasted_iota(jnp.int32, shape, 0)
    cell = lax.broadcasted_iota(jnp.int32, shape, 1)
    dy = (at // 16) - (cell // 16) - WIN
    dx = (at % 16) - (cell % 8) - WIN
    valid = (jnp.abs(dy) <= WIN) & (jnp.abs(dx) <= WIN)
    far = (dy.astype(jnp.float32) - shift_row) ** 2 + (dx.astype(jnp.float32) - shift_col) ** 2
    prior_ref[...] = jnp.where(valid, far * (-PRIOR * LOG2E), LOW)


def widen_row(wide_ref, at, row):
    row = row.astype(jnp.float32)
    edge = jnp.zeros((WIN, row.shape[1]), jnp.float32)
    left = jnp.concatenate([edge, row[:-WIN]], axis=0)
    right = jnp.concatenate([row[WIN:], edge], axis=0)
    wide_ref[at] = jnp.concatenate([left, right], axis=1).astype(jnp.bfloat16)


def tile_flow(window, fixed, prior_ref):
    cell = lax.broadcasted_iota(jnp.int32, fixed.shape, 0)
    first = ((cell % 16) < 8).astype(jnp.float32).astype(jnp.bfloat16)
    both = jnp.concatenate([fixed * first, fixed * (jnp.bfloat16(1.0) - first)], axis=1)
    corr = lax.dot_general(
        window, both, (((1,), (1,)), ((), ())), preferred_element_type=jnp.float32
    )
    scores = corr * (LOG2E / math.sqrt(fixed.shape[1])) + prior_ref[...]
    weights = jnp.exp2(scores - jnp.max(scores, axis=0, keepdims=True)).reshape(16, 16, 128)
    down = weights[15]
    rows = down
    for at in range(14, 0, -1):
        down = down + weights[at]
        rows = rows + down
    down = down + weights[0]
    inverse = 1.0 / jnp.sum(down, axis=0, keepdims=True)
    at = lax.broadcasted_iota(jnp.int32, (16, 128), 0).astype(jnp.float32)
    cell = lax.broadcasted_iota(jnp.int32, (1, 128), 1)
    flow_row = jnp.sum(rows, axis=0, keepdims=True) * inverse
    flow_col = jnp.sum(down * at, axis=0, keepdims=True) * inverse
    return (
        flow_row - ((cell // 16) + WIN).astype(jnp.float32),
        flow_col - ((cell % 8) + WIN).astype(jnp.float32),
    )


def flow_group(wide, fixed_rows, prior, out_ref, g):
    flow_rows, flow_cols = [], []
    top = pl.multiple_of(g * 8, 8)
    for j in range(wide.shape[1] // 16):
        window = wide[pl.ds(top, 16), 16 * j : 16 * j + 16, :].reshape(256, 256)
        fixed = fixed_rows(top, 16 * j).reshape(128, 128)
        flow_row, flow_col = tile_flow(window, fixed, prior)
        flow_rows.append(flow_row)
        flow_cols.append(flow_col)
    out_ref[0, g] = jnp.concatenate(flow_rows, axis=0)
    out_ref[1, g] = jnp.concatenate(flow_cols, axis=0)


def block_transpose(block):
    row = lax.broadcasted_iota(jnp.int32, block.shape, 0)
    part = lax.broadcasted_iota(jnp.int32, block.shape, 1) // 16
    for bit in (1, 2, 4):
        in_row, in_part = (row & bit) != 0, (part & bit) != 0
        down = pltpu.roll(pltpu.roll(block, bit, 0), 128 - 16 * bit, 1)
        up = pltpu.roll(pltpu.roll(block, 8 - bit, 0), 16 * bit, 1)
        block = jnp.where(in_row == in_part, block, jnp.where(in_row, down, up))
    return block


def loop(start, stop, step):
    def run(at, carry):
        step(at)
        return carry

    lax.fori_loop(start, stop, run, 0)


def kernel(
    secs, tiles, desc_far, steps_far, out,
    desc, steps, load_sem, steps_sem, sending, incoming, coarse, coarse_out, coarse_in, padded, near_edge, far_edge, wide, prior, near, far,
    main_send, main_recv, near_send, near_recv, far_send, far_recv,
    gather_send, gather_recv, hop_send, hop_recv, spread_send, spread_recv,
):
    rows = desc.shape[1]
    chunks = rows // POOL
    i, t = lax.axis_index("sec"), lax.axis_index("tile")
    gives, takes = i > 0, i < secs - 1

    def load(k):
        part = pl.ds(pl.multiple_of(k * POOL, POOL), POOL)
        return pltpu.make_async_copy(desc_far.at[:, part], desc.at[:, part], load_sem.at[k])

    steps_load = pltpu.make_async_copy(steps_far, steps, steps_sem)
    steps_load.start()
    load(0).start()
    load(chunks - 1).start()
    loop(1, chunks - 1, lambda k: load(k).start())

    def peer(d):
        return lax.rem(t + d, tiles)

    def remote(src, dst, send, recv, target):
        return pltpu.make_async_remote_copy(
            src_ref=src, dst_ref=dst, send_sem=send, recv_sem=recv,
            device_id=target, device_id_type=pl.DeviceIdType.MESH,
        )

    def main_copy(k):
        part = pl.ds(pl.multiple_of(k * POOL, POOL), POOL)
        return remote(
            sending.at[part], incoming.at[part], main_send.at[k], main_recv.at[k], {"sec": i - 1}
        )

    def gather_copy(d):
        slot = coarse.at[:, t]
        return remote(slot, slot, gather_send.at[d], gather_recv.at[d], {"tile": peer(d)})

    def hop_copy():
        return remote(coarse_out, coarse_in.at[t], hop_send, hop_recv, {"sec": i - 1})

    def spread_copy(d):
        slot = coarse_in.at[t]
        return remote(slot, slot, spread_send.at[d], spread_recv.at[d], {"tile": peer(d)})

    def edge_copy(source, edge, sems, side):
        part = source.at[rows - WIN :] if side == 0 else source.at[:WIN]
        target = t + 1 if side == 0 else t - 1
        return remote(part, edge.at[side], sems[0].at[side], sems[1].at[side], {"tile": target})

    near_sems, far_sems = (near_send, near_recv), (far_send, far_recv)
    near_source = desc.at[1]
    has_low, has_high = t > 0, t < tiles - 1

    def start_edges(source, edge, sems):
        pl.when(has_high)(lambda: edge_copy(source, edge, sems, 0).start())
        pl.when(has_low)(lambda: edge_copy(source, edge, sems, 1).start())

    def finish_edges(source, edge, sems):
        pl.when(has_high)(lambda: edge_copy(source, edge, sems, 0).wait_send())
        pl.when(has_low)(lambda: edge_copy(source, edge, sems, 1).wait_send())

    def receive_edges(source, edge, sems):
        pl.when(has_low)(lambda: edge_copy(source, edge, sems, 0).wait_recv())
        pl.when(has_high)(lambda: edge_copy(source, edge, sems, 1).wait_recv())

        @pl.when(t == 0)
        def _():
            edge[0] = jnp.zeros(edge.shape[1:], edge.dtype)

        @pl.when(t == tiles - 1)
        def _():
            edge[1] = jnp.zeros(edge.shape[1:], edge.dtype)

        for r in range(WIN):
            widen_row(wide, r, edge[0, r])
            widen_row(wide, rows + WIN + r, edge[1, r])

    barrier = pltpu.get_barrier_semaphore()

    def greet(target):
        pl.semaphore_signal(barrier, inc=1, device_id=target, device_id_type=pl.DeviceIdType.MESH)

    for d in range(1, tiles):
        greet({"tile": peer(d)})
    pl.when(gives)(lambda: greet({"sec": i - 1}))
    pl.when(takes)(lambda: greet({"sec": i + 1}))

    padded[...] = jnp.zeros(padded.shape, padded.dtype)
    steps_load.wait()
    own_first, own_second = steps[2 * i], steps[2 * i + 1]
    chosen = jnp.where(steps[jnp.maximum(2 * i - 1, 0)] == 2, 1, 0)
    sender = jnp.where(own_second > 0, 1, 0)

    def fill(k):
        for r in range(POOL):
            sending[k * POOL + r] = desc[chosen, k * POOL + r]

    load(0).wait()
    load(chunks - 1).wait()
    loop(1, chunks - 1, lambda k: load(k).wait())
    fill(0)
    fill(chunks - 1)
    pl.semaphore_wait(barrier, tiles - 1 + jnp.where(gives, 1, 0) + jnp.where(takes, 1, 0))

    @pl.when(gives)
    def _():
        main_copy(0).start()
        main_copy(chunks - 1).start()

    start_edges(near_source, near_edge, near_sems)

    def pool(k):
        means = []
        for s in range(2):
            summed = desc[s, k * POOL].astype(jnp.float32)
            for r in range(1, POOL):
                summed = summed + desc[s, k * POOL + r].astype(jnp.float32)
            summed = jnp.sum(summed.reshape(16, POOL, summed.shape[1]), axis=1)
            means.append(summed * (1.0 / (POOL * POOL)))
            coarse[s, t, k] = means[s].astype(jnp.bfloat16)
        coarse_out[k] = jnp.where(chosen == 0, means[0], means[1]).astype(jnp.bfloat16)

    loop(0, chunks, pool)
    for d in range(1, tiles):
        gather_copy(d).start()

    @pl.when(gives)
    def _():
        hop_copy().start()

    def pass_on(k):
        fill(k)
        pl.when(gives)(lambda: main_copy(k).start())

    loop(1, chunks - 1, pass_on)
    total = tiles * chunks
    loop(0, rows, lambda r: widen_row(wide, r + WIN, desc[1, r]))
    for d in range(1, tiles):
        gather_copy(d).wait_recv()

    @pl.when(takes)
    def _():
        hop_copy().wait_recv()
        for d in range(1, tiles):
            spread_copy(d).start()

    def lay(entry):
        for at in range(tiles):
            for k in range(chunks):
                padded[WIN + at * chunks + k] = entry(at, k)

    lay(lambda at, k: coarse[1, at, k])
    shift_row, shift_col = coarse_shift(lambda y: coarse[0, y // chunks, y % chunks], padded, total)
    fill_prior(prior, shift_row, shift_col)
    receive_edges(near_source, near_edge, near_sems)

    @pl.when(takes)
    def _():
        main_copy(0).wait_recv()
        main_copy(chunks - 1).wait_recv()
        start_edges(incoming, far_edge, far_sems)

    loop(
        0, chunks,
        lambda g: flow_group(wide, lambda top, col: desc[0, pl.ds(top, 8), col : col + 16, :], prior, near, g),
    )

    @pl.when(takes)
    def _():
        for r in range(POOL):
            widen_row(wide, r + WIN, incoming[r])
            widen_row(wide, rows - POOL + r + WIN, incoming[rows - POOL + r])
        for d in range(1, tiles):
            spread_copy(d).wait_recv()
        lay(lambda at, k: coarse_in[at, k])
        shift_row, shift_col = coarse_shift(lambda y: coarse[sender, y // chunks, y % chunks], padded, total)
        fill_prior(prior, shift_row, shift_col)
        receive_edges(incoming, far_edge, far_sems)

        def group(g):
            @pl.when(g < chunks - 2)
            def _():
                main_copy(g + 1).wait_recv()
                first = (g + 1) * POOL
                for r in range(POOL):
                    widen_row(wide, first + r + WIN, incoming[first + r])

            flow_group(wide, lambda top, col: desc[sender, pl.ds(top, 8), col : col + 16, :], prior, far, g)

        loop(0, chunks, group)
        for d in range(1, tiles):
            spread_copy(d).wait_send()
        finish_edges(incoming, far_edge, far_sems)

    @pl.when(i == secs - 1)
    def _():
        far[...] = jnp.zeros(far.shape, far.dtype)

    def write(g):
        part = pl.ds(pl.multiple_of(g * POOL, POOL), POOL)
        for c in range(2):
            first = jnp.where(own_first == 1, near[c, g], jnp.where(own_first == 2, far[c, g], 0.0))
            out[0, c, part] = block_transpose(first)
            out[1, c, part] = block_transpose(jnp.where(own_second > 0, far[c, g], 0.0))

    loop(0, chunks, write)
    for d in range(1, tiles):
        gather_copy(d).wait_send()
    finish_edges(near_source, near_edge, near_sems)

    @pl.when(gives)
    def _():
        hop_copy().wait_send()
        loop(0, chunks, lambda k: main_copy(k).wait_send())


def body(descriptors, partner_step):
    sections, rows, cols, depth = descriptors.shape
    secs, tiles = lax.axis_size("sec"), lax.axis_size("tile")
    chunks = rows // POOL
    narrow = jnp.bfloat16
    dma = pltpu.SemaphoreType.DMA
    result = (2, chunks, cols // 16, 128)
    return pl.pallas_call(
        functools.partial(kernel, secs, tiles),
        out_shape=jax.ShapeDtypeStruct((sections, 2, rows, cols), jnp.float32),
        in_specs=[pl.BlockSpec(memory_space=pltpu.HBM), pl.BlockSpec(memory_space=pltpu.HBM)],
        out_specs=pl.BlockSpec(memory_space=pltpu.VMEM),
        scratch_shapes=[
            pltpu.VMEM((sections, rows, cols, depth), narrow),
            pltpu.SMEM(partner_step.shape, jnp.int32),
            dma((chunks,)), dma,
            pltpu.VMEM((rows, cols, depth), narrow),
            pltpu.VMEM((rows, cols, depth), narrow),
            pltpu.VMEM((sections, tiles, chunks, 16, depth), narrow),
            pltpu.VMEM((chunks, 16, depth), narrow),
            pltpu.VMEM((tiles, chunks, 16, depth), narrow),
            pltpu.VMEM((tiles * chunks + 16, 16, depth), narrow),
            pltpu.VMEM((2, WIN, cols, depth), narrow),
            pltpu.VMEM((2, WIN, cols, depth), narrow),
            pltpu.VMEM((rows + 2 * WIN, cols, 2 * depth), narrow),
            pltpu.VMEM((256, 128), jnp.float32),
            pltpu.VMEM(result, jnp.float32),
            pltpu.VMEM(result, jnp.float32),
            dma((chunks,)), dma((chunks,)), dma((2,)), dma((2,)), dma((2,)), dma((2,)),
            dma((tiles,)), dma((tiles,)), dma, dma, dma((tiles,)), dma((tiles,)),
        ],
        compiler_params=pltpu.CompilerParams(
            vmem_limit_bytes=52 * 2**20, collective_id=0, has_side_effects=True
        ),
        cost_estimate=pl.CostEstimate(
            flops=4 * 256 * 256 * rows * cols, bytes_accessed=2**22, transcendentals=512 * rows * cols
        ),
    )(descriptors, partner_step)


def solution(mesh):
    return jax.shard_map(
        body,
        mesh=mesh,
        in_specs=(P("sec", "tile", None, None), P()),
        out_specs=P("sec", None, "tile", None),
        check_vma=False,
    )
```

```python
import functools
import math

import jax
import jax.numpy as jnp
from jax import lax
from jax.experimental import pallas as pl
from jax.experimental.pallas import tpu as pltpu
from jax.sharding import PartitionSpec as P

WIN = 4
POOL = 8
SIDE = 2 * WIN + 1
PRIOR = 0.25
LOG2E = math.log2(math.e)
LOW = -1e30


def coarse_shift(fixed_row, padded_ref, count):
    cols, depth = padded_ref.shape[1:]
    lanes = 16 * cols
    table = jnp.zeros((cols, lanes), jnp.float32)
    for y in range(0, count, 2):
        fixed = jnp.concatenate([fixed_row(y), fixed_row(y + 1)], axis=1)
        window = jnp.concatenate(
            [padded_ref[y + k : y + k + 16].reshape(lanes, depth) for k in (0, 1)], axis=1
        )
        table = table + lax.dot_general(
            fixed, window, (((1,), (1,)), ((), ())), preferred_element_type=jnp.float32
        )
    row = lax.broadcasted_iota(jnp.int32, (cols, lanes), 0)
    lane = lax.broadcasted_iota(jnp.int32, (cols, lanes), 1)
    table = jnp.where(jnp.abs(lane % cols - row) <= WIN, table, 0.0)
    for bit in (1, 2, 4, 8):
        table = jnp.where((row & bit) != 0, pltpu.roll(table, lanes - bit, 1), table)
    scores = jnp.sum(table, axis=0, keepdims=True) * (1.0 / math.sqrt(depth * count * cols))
    lane = lax.broadcasted_iota(jnp.int32, (1, lanes), 1) + cols // 2
    lane = jnp.where(lane >= lanes, lane - lanes, lane)
    dy = (lane // cols) - WIN
    dx = (lane % cols) - cols // 2
    valid = (dy <= WIN) & (jnp.abs(dx) <= WIN)
    scores = jnp.where(valid, scores, LOW)
    weights = jnp.exp(scores - jnp.max(scores, axis=1, keepdims=True))
    total = jnp.sum(weights, axis=1, keepdims=True)
    return (
        jnp.sum(weights * dy.astype(jnp.float32), axis=1, keepdims=True) / total,
        jnp.sum(weights * dx.astype(jnp.float32), axis=1, keepdims=True) / total,
    )


def fill_prior(prior_ref, shift_row, shift_col):
    shape = (256, 128)
    at = lax.broadcasted_iota(jnp.int32, shape, 0)
    cell = lax.broadcasted_iota(jnp.int32, shape, 1)
    dy = (at // 16) - (cell // 16) - WIN
    dx = (at % 16) - (cell % 8) - WIN
    valid = (jnp.abs(dy) <= WIN) & (jnp.abs(dx) <= WIN)
    far = (dy.astype(jnp.float32) - shift_row) ** 2 + (dx.astype(jnp.float32) - shift_col) ** 2
    prior_ref[...] = jnp.where(valid, far * (-PRIOR * LOG2E), LOW)


def widen_row(wide_ref, at, row):
    row = row.astype(jnp.float32)
    edge = jnp.zeros((WIN, row.shape[1]), jnp.float32)
    left = jnp.concatenate([edge, row[:-WIN]], axis=0)
    right = jnp.concatenate([row[WIN:], edge], axis=0)
    wide_ref[at] = jnp.concatenate([left, right], axis=1).astype(jnp.bfloat16)


def tile_flow(window, fixed, prior_ref):
    cell = lax.broadcasted_iota(jnp.int32, fixed.shape, 0)
    first = ((cell % 16) < 8).astype(jnp.float32).astype(jnp.bfloat16)
    both = jnp.concatenate([fixed * first, fixed * (jnp.bfloat16(1.0) - first)], axis=1)
    corr = lax.dot_general(
        window, both, (((1,), (1,)), ((), ())), preferred_element_type=jnp.float32
    )
    scores = corr * (LOG2E / math.sqrt(fixed.shape[1])) + prior_ref[...]
    weights = jnp.exp2(scores - jnp.max(scores, axis=0, keepdims=True)).reshape(16, 16, 128)
    down = weights[15]
    rows = down
    for at in range(14, 0, -1):
        down = down + weights[at]
        rows = rows + down
    down = down + weights[0]
    inverse = 1.0 / jnp.sum(down, axis=0, keepdims=True)
    at = lax.broadcasted_iota(jnp.int32, (16, 128), 0).astype(jnp.float32)
    cell = lax.broadcasted_iota(jnp.int32, (1, 128), 1)
    flow_row = jnp.sum(rows, axis=0, keepdims=True) * inverse
    flow_col = jnp.sum(down * at, axis=0, keepdims=True) * inverse
    return (
        flow_row - ((cell // 16) + WIN).astype(jnp.float32),
        flow_col - ((cell % 8) + WIN).astype(jnp.float32),
    )


def flow_group(wide, fixed_rows, prior, out_ref, g):
    flow_rows, flow_cols = [], []
    top = pl.multiple_of(g * 8, 8)
    for j in range(wide.shape[1] // 16):
        window = wide[pl.ds(top, 16), 16 * j : 16 * j + 16, :].reshape(256, 256)
        fixed = fixed_rows(top, 16 * j).reshape(128, 128)
        flow_row, flow_col = tile_flow(window, fixed, prior)
        flow_rows.append(flow_row)
        flow_cols.append(flow_col)
    out_ref[0, g] = jnp.concatenate(flow_rows, axis=0)
    out_ref[1, g] = jnp.concatenate(flow_cols, axis=0)


def block_transpose(block):
    row = lax.broadcasted_iota(jnp.int32, block.shape, 0)
    part = lax.broadcasted_iota(jnp.int32, block.shape, 1) // 16
    for bit in (1, 2, 4):
        in_row, in_part = (row & bit) != 0, (part & bit) != 0
        down = pltpu.roll(pltpu.roll(block, bit, 0), 128 - 16 * bit, 1)
        up = pltpu.roll(pltpu.roll(block, 8 - bit, 0), 16 * bit, 1)
        block = jnp.where(in_row == in_part, block, jnp.where(in_row, down, up))
    return block


def loop(start, stop, step):
    def run(at, carry):
        step(at)
        return carry

    lax.fori_loop(start, stop, run, 0)


def kernel(
    secs, tiles, desc_far, steps_far, out,
    desc, steps, load_sem, steps_sem, sending, incoming, coarse, coarse_out, coarse_in, padded, near_edge, far_edge, wide, prior, near, far,
    main_send, main_recv, near_send, near_recv, far_send, far_recv,
    gather_send, gather_recv, hop_send, hop_recv, spread_send, spread_recv,
):
    rows = desc.shape[1]
    chunks = rows // POOL
    i, t = lax.axis_index("sec"), lax.axis_index("tile")
    gives, takes = i > 0, i < secs - 1

    def load(k):
        part = pl.ds(pl.multiple_of(k * POOL, POOL), POOL)
        return pltpu.make_async_copy(desc_far.at[:, part], desc.at[:, part], load_sem.at[k])

    steps_load = pltpu.make_async_copy(steps_far, steps, steps_sem)
    steps_load.start()
    load(0).start()
    load(chunks - 1).start()
    loop(1, chunks - 1, lambda k: load(k).start())

    def peer(d):
        return lax.rem(t + d, tiles)

    def remote(src, dst, send, recv, target):
        return pltpu.make_async_remote_copy(
            src_ref=src, dst_ref=dst, send_sem=send, recv_sem=recv,
            device_id=target, device_id_type=pl.DeviceIdType.MESH,
        )

    def rows_copy(first, size, k):
        part = pl.ds(first, size)
        return remote(
            sending.at[part], incoming.at[part], main_send.at[k], main_recv.at[k], {"sec": i - 1}
        )

    def main_copy(k):
        return rows_copy(pl.multiple_of(k * POOL, POOL), POOL, k)

    split = chunks - 2

    def half_copy(half):
        return rows_copy(split * POOL + half * (POOL // 2), POOL // 2, split if half == 0 else chunks)

    def gather_copy(d):
        slot = coarse.at[:, t]
        return remote(slot, slot, gather_send.at[d], gather_recv.at[d], {"tile": peer(d)})

    def hop_copy():
        return remote(coarse_out, coarse_in.at[t], hop_send, hop_recv, {"sec": i - 1})

    def spread_copy(d):
        slot = coarse_in.at[t]
        return remote(slot, slot, spread_send.at[d], spread_recv.at[d], {"tile": peer(d)})

    def edge_copy(source, edge, sems, side):
        part = source.at[rows - WIN :] if side == 0 else source.at[:WIN]
        target = t + 1 if side == 0 else t - 1
        return remote(part, edge.at[side], sems[0].at[side], sems[1].at[side], {"tile": target})

    near_sems, far_sems = (near_send, near_recv), (far_send, far_recv)
    near_source = desc.at[1]
    has_low, has_high = t > 0, t < tiles - 1

    def start_edges(source, edge, sems):
        pl.when(has_high)(lambda: edge_copy(source, edge, sems, 0).start())
        pl.when(has_low)(lambda: edge_copy(source, edge, sems, 1).start())

    def finish_edges(source, edge, sems):
        pl.when(has_high)(lambda: edge_copy(source, edge, sems, 0).wait_send())
        pl.when(has_low)(lambda: edge_copy(source, edge, sems, 1).wait_send())

    def receive_edges(source, edge, sems):
        pl.when(has_low)(lambda: edge_copy(source, edge, sems, 0).wait_recv())
        pl.when(has_high)(lambda: edge_copy(source, edge, sems, 1).wait_recv())

        @pl.when(t == 0)
        def _():
            edge[0] = jnp.zeros(edge.shape[1:], edge.dtype)

        @pl.when(t == tiles - 1)
        def _():
            edge[1] = jnp.zeros(edge.shape[1:], edge.dtype)

        for r in range(WIN):
            widen_row(wide, r, edge[0, r])
            widen_row(wide, rows + WIN + r, edge[1, r])

    barrier = pltpu.get_barrier_semaphore()

    def greet(target):
        pl.semaphore_signal(barrier, inc=1, device_id=target, device_id_type=pl.DeviceIdType.MESH)

    for d in range(1, tiles):
        greet({"tile": peer(d)})
    pl.when(gives)(lambda: greet({"sec": i - 1}))
    pl.when(takes)(lambda: greet({"sec": i + 1}))

    padded[...] = jnp.zeros(padded.shape, padded.dtype)
    steps_load.wait()
    own_first, own_second = steps[2 * i], steps[2 * i + 1]
    chosen = jnp.where(steps[jnp.maximum(2 * i - 1, 0)] == 2, 1, 0)
    sender = jnp.where(own_second > 0, 1, 0)

    def fill(k):
        for r in range(POOL):
            at = k * POOL + r
            sending[at] = jnp.where(chosen == 0, desc[0, at], desc[1, at])

    load(0).wait()
    fill(0)
    pl.semaphore_wait(barrier, tiles - 1 + jnp.where(gives, 1, 0) + jnp.where(takes, 1, 0))
    pl.when(gives)(lambda: main_copy(0).start())
    load(chunks - 1).wait()
    fill(chunks - 1)
    pl.when(gives)(lambda: main_copy(chunks - 1).start())
    loop(1, chunks - 1, lambda k: load(k).wait())

    def pool(k):
        means = []
        for s in range(2):
            summed = desc[s, k * POOL].astype(jnp.float32)
            for r in range(1, POOL):
                summed = summed + desc[s, k * POOL + r].astype(jnp.float32)
            summed = jnp.sum(summed.reshape(16, POOL, summed.shape[1]), axis=1)
            means.append(summed * (1.0 / (POOL * POOL)))
            coarse[s, t, k] = means[s].astype(jnp.bfloat16)
        coarse_out[k] = jnp.where(chosen == 0, means[0], means[1]).astype(jnp.bfloat16)

    loop(0, chunks, pool)
    for d in range(1, tiles):
        gather_copy(d).start()

    @pl.when(gives)
    def _():
        hop_copy().start()

    start_edges(near_source, near_edge, near_sems)

    def pass_on(k):
        fill(k)
        pl.when(gives)(lambda: main_copy(k).start())

    loop(1, split, pass_on)
    fill(split)

    @pl.when(gives)
    def _():
        half_copy(0).start()
        half_copy(1).start()

    total = tiles * chunks
    loop(0, rows, lambda r: widen_row(wide, r + WIN, desc[1, r]))
    for d in range(1, tiles):
        gather_copy(d).wait_recv()

    @pl.when(takes)
    def _():
        hop_copy().wait_recv()
        for d in range(1, tiles):
            spread_copy(d).start()

    def lay(entry):
        for at in range(tiles):
            for k in range(chunks):
                padded[WIN + at * chunks + k] = entry(at, k)

    lay(lambda at, k: coarse[1, at, k])
    shift_row, shift_col = coarse_shift(lambda y: coarse[0, y // chunks, y % chunks], padded, total)
    fill_prior(prior, shift_row, shift_col)
    receive_edges(near_source, near_edge, near_sems)

    @pl.when(takes)
    def _():
        main_copy(0).wait_recv()
        main_copy(chunks - 1).wait_recv()
        start_edges(incoming, far_edge, far_sems)

    loop(
        0, chunks,
        lambda g: flow_group(wide, lambda top, col: desc[0, pl.ds(top, 8), col : col + 16, :], prior, near, g),
    )

    def write(g):
        part = pl.ds(pl.multiple_of(g * POOL, POOL), POOL)
        for c in range(2):
            first = jnp.where(own_first == 1, near[c, g], jnp.where(own_first == 2, far[c, g], 0.0))
            out[0, c, part] = block_transpose(first)
            out[1, c, part] = block_transpose(jnp.where(own_second > 0, far[c, g], 0.0))

    @pl.when(takes)
    def _():
        for r in range(POOL):
            widen_row(wide, r + WIN, incoming[r])
            widen_row(wide, rows - POOL + r + WIN, incoming[rows - POOL + r])
        for d in range(1, tiles):
            spread_copy(d).wait_recv()
        lay(lambda at, k: coarse_in[at, k])
        shift_row, shift_col = coarse_shift(lambda y: coarse[sender, y // chunks, y % chunks], padded, total)
        fill_prior(prior, shift_row, shift_col)
        receive_edges(incoming, far_edge, far_sems)

        def widen_half(half):
            half_copy(half).wait_recv()
            first = split * POOL + half * (POOL // 2)
            for r in range(POOL // 2):
                widen_row(wide, first + r + WIN, incoming[first + r])

        def group(g):
            @pl.when(g + 1 < split)
            def _():
                main_copy(g + 1).wait_recv()
                first = (g + 1) * POOL
                for r in range(POOL):
                    widen_row(wide, first + r + WIN, incoming[first + r])

            pl.when(g + 1 == split)(lambda: widen_half(0))
            pl.when(g == split)(lambda: widen_half(1))
            flow_group(wide, lambda top, col: desc[sender, pl.ds(top, 8), col : col + 16, :], prior, far, g)
            write(g)

        loop(0, chunks, group)
        for d in range(1, tiles):
            spread_copy(d).wait_send()
        finish_edges(incoming, far_edge, far_sems)

    @pl.when(i == secs - 1)
    def _():
        far[...] = jnp.zeros(far.shape, far.dtype)
        loop(0, chunks, write)

    for d in range(1, tiles):
        gather_copy(d).wait_send()
    finish_edges(near_source, near_edge, near_sems)

    @pl.when(gives)
    def _():
        hop_copy().wait_send()
        loop(0, split, lambda k: main_copy(k).wait_send())
        main_copy(chunks - 1).wait_send()
        half_copy(0).wait_send()
        half_copy(1).wait_send()


def body(descriptors, partner_step):
    sections, rows, cols, depth = descriptors.shape
    secs, tiles = lax.axis_size("sec"), lax.axis_size("tile")
    chunks = rows // POOL
    narrow = jnp.bfloat16
    dma = pltpu.SemaphoreType.DMA
    result = (2, chunks, cols // 16, 128)
    return pl.pallas_call(
        functools.partial(kernel, secs, tiles),
        out_shape=jax.ShapeDtypeStruct((sections, 2, rows, cols), jnp.float32),
        in_specs=[pl.BlockSpec(memory_space=pltpu.HBM), pl.BlockSpec(memory_space=pltpu.HBM)],
        out_specs=pl.BlockSpec(memory_space=pltpu.VMEM),
        scratch_shapes=[
            pltpu.VMEM((sections, rows, cols, depth), narrow),
            pltpu.SMEM(partner_step.shape, jnp.int32),
            dma((chunks,)), dma,
            pltpu.VMEM((rows, cols, depth), narrow),
            pltpu.VMEM((rows, cols, depth), narrow),
            pltpu.VMEM((sections, tiles, chunks, 16, depth), narrow),
            pltpu.VMEM((chunks, 16, depth), narrow),
            pltpu.VMEM((tiles, chunks, 16, depth), narrow),
            pltpu.VMEM((tiles * chunks + 16, 16, depth), narrow),
            pltpu.VMEM((2, WIN, cols, depth), narrow),
            pltpu.VMEM((2, WIN, cols, depth), narrow),
            pltpu.VMEM((rows + 2 * WIN, cols, 2 * depth), narrow),
            pltpu.VMEM((256, 128), jnp.float32),
            pltpu.VMEM(result, jnp.float32),
            pltpu.VMEM(result, jnp.float32),
            dma((chunks + 1,)), dma((chunks + 1,)), dma((2,)), dma((2,)), dma((2,)), dma((2,)),
            dma((tiles,)), dma((tiles,)), dma, dma, dma((tiles,)), dma((tiles,)),
        ],
        compiler_params=pltpu.CompilerParams(
            vmem_limit_bytes=52 * 2**20, collective_id=0, has_side_effects=True
        ),
        cost_estimate=pl.CostEstimate(
            flops=4 * 256 * 256 * rows * cols, bytes_accessed=2**22, transcendentals=512 * rows * cols
        ),
    )(descriptors, pltpu.with_memory_space_constraint(partner_step, pltpu.HBM))


def solution(mesh):
    return jax.shard_map(
        body,
        mesh=mesh,
        in_specs=(P("sec", "tile", None, None), P()),
        out_specs=P("sec", None, "tile", None),
        check_vma=False,
    )
```

```python
import functools
import math

import jax
import jax.numpy as jnp
from jax import lax
from jax.experimental import pallas as pl
from jax.experimental.pallas import tpu as pltpu
from jax.sharding import PartitionSpec as P

WIN = 4
POOL = 8
SIDE = 2 * WIN + 1
PRIOR = 0.25
LOG2E = math.log2(math.e)
LOW = -1e30


def coarse_shift(fixed_row, padded_ref, count):
    cols, depth = padded_ref.shape[1:]
    lanes = 16 * cols
    table = jnp.zeros((cols, lanes), jnp.float32)
    for y in range(0, count, 2):
        fixed = jnp.concatenate([fixed_row(y), fixed_row(y + 1)], axis=1)
        window = jnp.concatenate(
            [padded_ref[y + k : y + k + 16].reshape(lanes, depth) for k in (0, 1)], axis=1
        )
        table = table + lax.dot_general(
            fixed, window, (((1,), (1,)), ((), ())), preferred_element_type=jnp.float32
        )
    row = lax.broadcasted_iota(jnp.int32, (cols, lanes), 0)
    lane = lax.broadcasted_iota(jnp.int32, (cols, lanes), 1)
    table = jnp.where(jnp.abs(lane % cols - row) <= WIN, table, 0.0)
    for bit in (1, 2, 4, 8):
        table = jnp.where((row & bit) != 0, pltpu.roll(table, lanes - bit, 1), table)
    scores = jnp.sum(table, axis=0, keepdims=True) * (1.0 / math.sqrt(depth * count * cols))
    lane = lax.broadcasted_iota(jnp.int32, (1, lanes), 1) + cols // 2
    lane = jnp.where(lane >= lanes, lane - lanes, lane)
    dy = (lane // cols) - WIN
    dx = (lane % cols) - cols // 2
    valid = (dy <= WIN) & (jnp.abs(dx) <= WIN)
    scores = jnp.where(valid, scores, LOW)
    weights = jnp.exp(scores - jnp.max(scores, axis=1, keepdims=True))
    total = jnp.sum(weights, axis=1, keepdims=True)
    return (
        jnp.sum(weights * dy.astype(jnp.float32), axis=1, keepdims=True) / total,
        jnp.sum(weights * dx.astype(jnp.float32), axis=1, keepdims=True) / total,
    )


def fill_prior(prior_ref, shift_row, shift_col):
    shape = (256, 128)
    at = lax.broadcasted_iota(jnp.int32, shape, 0)
    cell = lax.broadcasted_iota(jnp.int32, shape, 1)
    dy = (at // 16) - (cell // 16) - WIN
    dx = (at % 16) - (cell % 8) - WIN
    valid = (jnp.abs(dy) <= WIN) & (jnp.abs(dx) <= WIN)
    far = (dy.astype(jnp.float32) - shift_row) ** 2 + (dx.astype(jnp.float32) - shift_col) ** 2
    prior_ref[...] = jnp.where(valid, far * (-PRIOR * LOG2E), LOW)


def widen_row(wide_ref, at, row):
    row = row.astype(jnp.float32)
    edge = jnp.zeros((WIN, row.shape[1]), jnp.float32)
    left = jnp.concatenate([edge, row[:-WIN]], axis=0)
    right = jnp.concatenate([row[WIN:], edge], axis=0)
    wide_ref[at] = jnp.concatenate([left, right], axis=1).astype(jnp.bfloat16)


def tile_flow(window, fixed, prior_ref):
    cell = lax.broadcasted_iota(jnp.int32, fixed.shape, 0)
    first = ((cell % 16) < 8).astype(jnp.float32).astype(jnp.bfloat16)
    both = jnp.concatenate([fixed * first, fixed * (jnp.bfloat16(1.0) - first)], axis=1)
    corr = lax.dot_general(
        window, both, (((1,), (1,)), ((), ())), preferred_element_type=jnp.float32
    )
    scores = corr * (LOG2E / math.sqrt(fixed.shape[1])) + prior_ref[...]
    weights = jnp.exp2(scores - jnp.max(scores, axis=0, keepdims=True)).reshape(16, 16, 128)
    down = weights[15]
    rows = down
    for at in range(14, 0, -1):
        down = down + weights[at]
        rows = rows + down
    down = down + weights[0]
    inverse = 1.0 / jnp.sum(down, axis=0, keepdims=True)
    at = lax.broadcasted_iota(jnp.int32, (16, 128), 0).astype(jnp.float32)
    cell = lax.broadcasted_iota(jnp.int32, (1, 128), 1)
    flow_row = jnp.sum(rows, axis=0, keepdims=True) * inverse
    flow_col = jnp.sum(down * at, axis=0, keepdims=True) * inverse
    return (
        flow_row - ((cell // 16) + WIN).astype(jnp.float32),
        flow_col - ((cell % 8) + WIN).astype(jnp.float32),
    )


def flow_group(wide, fixed_rows, prior, out_ref, g):
    flow_rows, flow_cols = [], []
    top = pl.multiple_of(g * 8, 8)
    for j in range(wide.shape[1] // 16):
        window = wide[pl.ds(top, 16), 16 * j : 16 * j + 16, :].reshape(256, 256)
        fixed = fixed_rows(top, 16 * j).reshape(128, 128)
        flow_row, flow_col = tile_flow(window, fixed, prior)
        flow_rows.append(flow_row)
        flow_cols.append(flow_col)
    out_ref[0, g] = jnp.concatenate(flow_rows, axis=0)
    out_ref[1, g] = jnp.concatenate(flow_cols, axis=0)


def block_transpose(block):
    row = lax.broadcasted_iota(jnp.int32, block.shape, 0)
    part = lax.broadcasted_iota(jnp.int32, block.shape, 1) // 16
    for bit in (1, 2, 4):
        in_row, in_part = (row & bit) != 0, (part & bit) != 0
        down = pltpu.roll(pltpu.roll(block, bit, 0), 128 - 16 * bit, 1)
        up = pltpu.roll(pltpu.roll(block, 8 - bit, 0), 16 * bit, 1)
        block = jnp.where(in_row == in_part, block, jnp.where(in_row, down, up))
    return block


def loop(start, stop, step):
    def run(at, carry):
        step(at)
        return carry

    lax.fori_loop(start, stop, run, 0)


def kernel(
    secs, tiles, desc_far, steps_far, out,
    desc, steps, load_sem, steps_sem, sending, incoming, coarse, coarse_out, coarse_in, padded, near_edge, far_edge, wide, prior, near, far,
    main_send, main_recv, near_send, near_recv, far_send, far_recv,
    gather_send, gather_recv, hop_send, hop_recv, spread_send, spread_recv,
):
    rows = desc.shape[1]
    chunks = rows // POOL
    i, t = lax.axis_index("sec"), lax.axis_index("tile")
    gives, takes = i > 0, i < secs - 1

    def peer(d):
        return lax.rem(t + d, tiles)

    barrier = pltpu.get_barrier_semaphore()

    def greet(target):
        pl.semaphore_signal(barrier, inc=1, device_id=target, device_id_type=pl.DeviceIdType.MESH)

    pl.when(gives)(lambda: greet({"sec": i - 1}))
    pl.when(takes)(lambda: greet({"sec": i + 1}))
    for d in range(1, tiles):
        greet({"tile": peer(d)})

    def load(k):
        part = pl.ds(pl.multiple_of(k * POOL, POOL), POOL)
        return pltpu.make_async_copy(desc_far.at[:, part], desc.at[:, part], load_sem.at[k])

    steps_load = pltpu.make_async_copy(steps_far, steps, steps_sem)
    steps_load.start()
    load(0).start()
    load(chunks - 1).start()
    loop(1, chunks - 1, lambda k: load(k).start())

    def remote(src, dst, send, recv, target):
        return pltpu.make_async_remote_copy(
            src_ref=src, dst_ref=dst, send_sem=send, recv_sem=recv,
            device_id=target, device_id_type=pl.DeviceIdType.MESH,
        )

    def rows_copy(first, size, k):
        part = pl.ds(first, size)
        return remote(
            sending.at[part], incoming.at[part], main_send.at[k], main_recv.at[k], {"sec": i - 1}
        )

    def main_copy(k):
        return rows_copy(pl.multiple_of(k * POOL, POOL), POOL, k)

    split = chunks - 2

    def half_copy(half):
        return rows_copy(split * POOL + half * (POOL // 2), POOL // 2, split if half == 0 else chunks)

    def gather_copy(d):
        slot = coarse.at[:, t]
        return remote(slot, slot, gather_send.at[d], gather_recv.at[d], {"tile": peer(d)})

    def hop_copy():
        return remote(coarse_out, coarse_in.at[t], hop_send, hop_recv, {"sec": i - 1})

    def spread_copy(d):
        slot = coarse_in.at[t]
        return remote(slot, slot, spread_send.at[d], spread_recv.at[d], {"tile": peer(d)})

    def edge_copy(source, edge, sems, side):
        part = source.at[rows - WIN :] if side == 0 else source.at[:WIN]
        target = t + 1 if side == 0 else t - 1
        return remote(part, edge.at[side], sems[0].at[side], sems[1].at[side], {"tile": target})

    near_sems, far_sems = (near_send, near_recv), (far_send, far_recv)
    near_source = desc.at[1]
    has_low, has_high = t > 0, t < tiles - 1

    def start_edges(source, edge, sems):
        pl.when(has_high)(lambda: edge_copy(source, edge, sems, 0).start())
        pl.when(has_low)(lambda: edge_copy(source, edge, sems, 1).start())

    def finish_edges(source, edge, sems):
        pl.when(has_high)(lambda: edge_copy(source, edge, sems, 0).wait_send())
        pl.when(has_low)(lambda: edge_copy(source, edge, sems, 1).wait_send())

    def receive_edges(source, edge, sems):
        pl.when(has_low)(lambda: edge_copy(source, edge, sems, 0).wait_recv())
        pl.when(has_high)(lambda: edge_copy(source, edge, sems, 1).wait_recv())

        @pl.when(t == 0)
        def _():
            edge[0] = jnp.zeros(edge.shape[1:], edge.dtype)

        @pl.when(t == tiles - 1)
        def _():
            edge[1] = jnp.zeros(edge.shape[1:], edge.dtype)

        for r in range(WIN):
            widen_row(wide, r, edge[0, r])
            widen_row(wide, rows + WIN + r, edge[1, r])

    padded[...] = jnp.zeros(padded.shape, padded.dtype)
    steps_load.wait()
    own_first, own_second = steps[2 * i], steps[2 * i + 1]
    chosen = jnp.where(steps[jnp.maximum(2 * i - 1, 0)] == 2, 1, 0)
    sender = jnp.where(own_second > 0, 1, 0)

    def fill(k):
        for r in range(POOL):
            at = k * POOL + r
            sending[at] = jnp.where(chosen == 0, desc[0, at], desc[1, at])

    load(0).wait()
    fill(0)
    pl.semaphore_wait(barrier, tiles - 1 + jnp.where(gives, 1, 0) + jnp.where(takes, 1, 0))
    pl.when(gives)(lambda: main_copy(0).start())
    load(chunks - 1).wait()
    fill(chunks - 1)
    pl.when(gives)(lambda: main_copy(chunks - 1).start())
    loop(1, chunks - 1, lambda k: load(k).wait())

    def pool(k):
        means = []
        for s in range(2):
            summed = desc[s, k * POOL].astype(jnp.float32)
            for r in range(1, POOL):
                summed = summed + desc[s, k * POOL + r].astype(jnp.float32)
            summed = jnp.sum(summed.reshape(16, POOL, summed.shape[1]), axis=1)
            means.append(summed * (1.0 / (POOL * POOL)))
            coarse[s, t, k] = means[s].astype(jnp.bfloat16)
        coarse_out[k] = jnp.where(chosen == 0, means[0], means[1]).astype(jnp.bfloat16)

    loop(0, chunks, pool)
    for d in range(1, tiles):
        gather_copy(d).start()

    @pl.when(gives)
    def _():
        hop_copy().start()

    start_edges(near_source, near_edge, near_sems)

    def pass_on(k):
        fill(k)
        pl.when(gives)(lambda: main_copy(k).start())

    loop(1, split, pass_on)
    fill(split)

    @pl.when(gives)
    def _():
        half_copy(0).start()
        half_copy(1).start()

    total = tiles * chunks
    loop(0, rows, lambda r: widen_row(wide, r + WIN, desc[1, r]))
    for d in range(1, tiles):
        gather_copy(d).wait_recv()

    @pl.when(takes)
    def _():
        hop_copy().wait_recv()
        for d in range(1, tiles):
            spread_copy(d).start()

    def lay(entry):
        for at in range(tiles):
            for k in range(chunks):
                padded[WIN + at * chunks + k] = entry(at, k)

    lay(lambda at, k: coarse[1, at, k])
    shift_row, shift_col = coarse_shift(lambda y: coarse[0, y // chunks, y % chunks], padded, total)
    fill_prior(prior, shift_row, shift_col)
    receive_edges(near_source, near_edge, near_sems)

    @pl.when(takes)
    def _():
        main_copy(0).wait_recv()
        main_copy(chunks - 1).wait_recv()
        start_edges(incoming, far_edge, far_sems)

    loop(
        0, chunks,
        lambda g: flow_group(wide, lambda top, col: desc[0, pl.ds(top, 8), col : col + 16, :], prior, near, g),
    )

    def write(g):
        part = pl.ds(pl.multiple_of(g * POOL, POOL), POOL)
        for c in range(2):
            first = jnp.where(own_first == 1, near[c, g], jnp.where(own_first == 2, far[c, g], 0.0))
            out[0, c, part] = block_transpose(first)
            out[1, c, part] = block_transpose(jnp.where(own_second > 0, far[c, g], 0.0))

    @pl.when(takes)
    def _():
        for r in range(POOL):
            widen_row(wide, r + WIN, incoming[r])
            widen_row(wide, rows - POOL + r + WIN, incoming[rows - POOL + r])
        for d in range(1, tiles):
            spread_copy(d).wait_recv()
        lay(lambda at, k: coarse_in[at, k])
        shift_row, shift_col = coarse_shift(lambda y: coarse[sender, y // chunks, y % chunks], padded, total)
        fill_prior(prior, shift_row, shift_col)
        receive_edges(incoming, far_edge, far_sems)

        def widen_half(half):
            half_copy(half).wait_recv()
            first = split * POOL + half * (POOL // 2)
            for r in range(POOL // 2):
                widen_row(wide, first + r + WIN, incoming[first + r])

        def group(g):
            @pl.when(g + 1 < split)
            def _():
                main_copy(g + 1).wait_recv()
                first = (g + 1) * POOL
                for r in range(POOL):
                    widen_row(wide, first + r + WIN, incoming[first + r])

            pl.when(g + 1 == split)(lambda: widen_half(0))
            pl.when(g == split)(lambda: widen_half(1))
            flow_group(wide, lambda top, col: desc[sender, pl.ds(top, 8), col : col + 16, :], prior, far, g)
            write(g)

        loop(0, chunks, group)
        for d in range(1, tiles):
            spread_copy(d).wait_send()
        finish_edges(incoming, far_edge, far_sems)

    @pl.when(i == secs - 1)
    def _():
        far[...] = jnp.zeros(far.shape, far.dtype)
        loop(0, chunks, write)

    for d in range(1, tiles):
        gather_copy(d).wait_send()
    finish_edges(near_source, near_edge, near_sems)

    @pl.when(gives)
    def _():
        hop_copy().wait_send()
        loop(0, split, lambda k: main_copy(k).wait_send())
        main_copy(chunks - 1).wait_send()
        half_copy(0).wait_send()
        half_copy(1).wait_send()


def body(descriptors, partner_step):
    sections, rows, cols, depth = descriptors.shape
    secs, tiles = lax.axis_size("sec"), lax.axis_size("tile")
    chunks = rows // POOL
    narrow = jnp.bfloat16
    dma = pltpu.SemaphoreType.DMA
    result = (2, chunks, cols // 16, 128)
    return pl.pallas_call(
        functools.partial(kernel, secs, tiles),
        out_shape=jax.ShapeDtypeStruct((sections, 2, rows, cols), jnp.float32),
        in_specs=[pl.BlockSpec(memory_space=pltpu.HBM), pl.BlockSpec(memory_space=pltpu.HBM)],
        out_specs=pl.BlockSpec(memory_space=pltpu.VMEM),
        scratch_shapes=[
            pltpu.VMEM((sections, rows, cols, depth), narrow),
            pltpu.SMEM(partner_step.shape, jnp.int32),
            dma((chunks,)), dma,
            pltpu.VMEM((rows, cols, depth), narrow),
            pltpu.VMEM((rows, cols, depth), narrow),
            pltpu.VMEM((sections, tiles, chunks, 16, depth), narrow),
            pltpu.VMEM((chunks, 16, depth), narrow),
            pltpu.VMEM((tiles, chunks, 16, depth), narrow),
            pltpu.VMEM((tiles * chunks + 16, 16, depth), narrow),
            pltpu.VMEM((2, WIN, cols, depth), narrow),
            pltpu.VMEM((2, WIN, cols, depth), narrow),
            pltpu.VMEM((rows + 2 * WIN, cols, 2 * depth), narrow),
            pltpu.VMEM((256, 128), jnp.float32),
            pltpu.VMEM(result, jnp.float32),
            pltpu.VMEM(result, jnp.float32),
            dma((chunks + 1,)), dma((chunks + 1,)), dma((2,)), dma((2,)), dma((2,)), dma((2,)),
            dma((tiles,)), dma((tiles,)), dma, dma, dma((tiles,)), dma((tiles,)),
        ],
        compiler_params=pltpu.CompilerParams(
            vmem_limit_bytes=52 * 2**20, collective_id=0, has_side_effects=True
        ),
        cost_estimate=pl.CostEstimate(
            flops=4 * 256 * 256 * rows * cols, bytes_accessed=2**22, transcendentals=512 * rows * cols
        ),
    )(descriptors, pltpu.with_memory_space_constraint(partner_step, pltpu.HBM))


def solution(mesh):
    return jax.shard_map(
        body,
        mesh=mesh,
        in_specs=(P("sec", "tile", None, None), P()),
        out_specs=P("sec", None, "tile", None),
        check_vma=False,
    )
```
